512 devices in a mesh: head: 16 (over y, x), seq: 32 (over z, core).
Axes of the slice: x: 4, y: 4, z: 16, core: 2. Of those that a mesh axis runs over, the one named last changes fastest.
Arguments:
- queries: bfloat16 [65536, 2048], P(('seq', 'head')), may hold values from -6 to 6
- key_vectors: bfloat16 [65536, 2048], P(('seq', 'head')), may hold values from -6 to 6
- value_vectors: bfloat16 [65536, 2048], P(('seq', 'head')), may hold values from -6 to 6
- cotangent: bfloat16 [65536, 2048], P(('seq', 'head')), may hold values from -6 to 6
Outputs:
- normed_out: bfloat16 [65536, 2048], P(('seq', 'head'))
- query_grad: bfloat16 [65536, 2048], P(('seq', 'head'))
- key_grad: bfloat16 [65536, 2048], P(('seq', 'head'))
- value_grad: bfloat16 [65536, 2048], P(('seq', 'head'))
The draws below stay inside these ranges and needn't reach their ends.
All inputs are finite; a program needn't handle non-finite values.
Results may differ from the reference program's by a relative error of at most 0.005.
Values may be sent and summed in bfloat16 or wider, within the bound.
A program may use at most 64 MiB of HBM per device.

```python
import jax
import jax.numpy as jnp
from jax import lax

H = 16
DH = 128
D = 2048
SLAB = 1024
SLABS = 64
TOKENS = 65536


def block_levels(rng, extent, cuts, smallest, largest):
    def one(axis_at, blocks):
        draws = jax.random.uniform(jax.random.fold_in(jax.random.fold_in(rng, 6), axis_at), (blocks,), jnp.float32, smallest / len(cuts), largest / len(cuts))
        return jnp.repeat(jnp.exp(draws), extent[axis_at] // blocks).reshape((-1,) + (1,) * (len(extent) - axis_at - 1))

    loudness = one(*cuts[0])
    for cut in cuts[1:]:
        loudness = loudness * one(*cut)
    return loudness


def noise(key, dims, width, limit, cuts=(), kind=jnp.bfloat16):
    loudness = block_levels(key, dims, cuts, -0.22, 0.18) if cuts else 1.0
    result = jax.random.normal(key, dims, jnp.float32) * width * loudness
    return jnp.minimum(jnp.maximum(result, -limit), limit).astype(kind)


def setup_inputs(seed: int = 0) -> dict:
    splits = jax.random.split(jax.random.key(seed), 5)
    queries = noise(splits[0], (TOKENS, D), 1.0, 6.0, ((0, 512),))
    key_vectors = noise(splits[1], (TOKENS, D), 1.0, 6.0, ((0, 512),))
    value_vectors = noise(splits[2], (TOKENS, D), 1.0, 6.0, ((0, 512),))
    cotangent = noise(splits[3], (TOKENS, D), 1.0, 6.0, ((0, 512),))
    return dict(queries=queries, key_vectors=key_vectors, value_vectors=value_vectors, cotangent=cotangent)


epsilon = 1e-06

def head_pass(blocks):
    q_all, k_all, v_all, g_all = blocks
    causal = jnp.tril(jnp.ones((SLAB, SLAB), dtype=bool))

    def forward_step(state, slab_in):
        q_blk, k_blk, v_blk, g_blk = slab_in
        slab_kv = jnp.dot(k_blk.T, v_blk, preferred_element_type=jnp.float32)
        scores = jnp.dot(q_blk, k_blk.T, preferred_element_type=jnp.float32)
        masked_scores = jnp.where(causal, scores, jnp.float32(0.0)).astype(jnp.bfloat16)
        attn_out = jnp.dot(masked_scores, v_blk, preferred_element_type=jnp.float32)
        attn_out = attn_out + jnp.dot(q_blk.astype(jnp.float32), state, precision=lax.Precision.HIGHEST)
        inv_rms = lax.rsqrt(lax.optimization_barrier(jnp.mean(attn_out * attn_out, axis=-1, keepdims=True)) + epsilon)
        normed = attn_out * inv_rms
        cot = g_blk.astype(jnp.float32)
        out_grad = (inv_rms * (cot - normed * lax.optimization_barrier(jnp.mean(cot * normed, axis=-1, keepdims=True)))).astype(jnp.bfloat16)
        slab_grad = jnp.dot(q_blk.T, out_grad, preferred_element_type=jnp.float32)
        grads = jnp.dot(out_grad, v_blk.T, preferred_element_type=jnp.float32)
        masked_grads = jnp.where(causal, grads, jnp.float32(0.0)).astype(jnp.bfloat16)
        query_grad = jnp.dot(masked_grads, k_blk, preferred_element_type=jnp.float32)
        query_grad = query_grad + jnp.dot(out_grad.astype(jnp.float32), state.T, precision=lax.Precision.HIGHEST)
        key_local = jnp.dot(masked_grads.T, q_blk, preferred_element_type=jnp.float32)
        value_local = jnp.dot(masked_scores.T, out_grad, preferred_element_type=jnp.float32)
        return (state + slab_kv, (normed.astype(jnp.bfloat16), query_grad.astype(jnp.bfloat16), key_local, value_local, slab_grad))
    start_state = jnp.zeros((DH, DH), jnp.float32)
    _, (normed_all, qgrad_all, key_local, value_local, slab_grads) = lax.scan(forward_step, start_state, (q_all, k_all, v_all, g_all))

    def backward_step(grad_state, slab_in):
        k_blk, v_blk, key_part, value_part, slab_grad = slab_in
        key_grad = key_part + jnp.dot(v_blk.astype(jnp.float32), grad_state.T, precision=lax.Precision.HIGHEST)
        value_grad = value_part + jnp.dot(k_blk.astype(jnp.float32), grad_state, precision=lax.Precision.HIGHEST)
        return (grad_state + slab_grad, (key_grad.astype(jnp.bfloat16), value_grad.astype(jnp.bfloat16)))
    _, (kgrad_all, vgrad_all) = lax.scan(backward_step, start_state, (k_all, v_all, key_local, value_local, slab_grads), reverse=True)
    return (normed_all, qgrad_all, kgrad_all, vgrad_all)

def to_heads(array):
    return jnp.transpose(array.reshape(SLABS, SLAB, H, DH), (2, 0, 1, 3))

def from_heads(array):
    return jnp.transpose(array, (1, 2, 0, 3)).reshape(TOKENS, H * DH)

def reference(queries, key_vectors, value_vectors, cotangent):
    inputs = (to_heads(queries), to_heads(key_vectors), to_heads(value_vectors), to_heads(cotangent))
    normed_all, qgrad_all, kgrad_all, vgrad_all = lax.map(head_pass, inputs)
    return (from_heads(normed_all), from_heads(qgrad_all), from_heads(kgrad_all), from_heads(vgrad_all))
```

```python
import jax
import jax.numpy as jnp
from jax import lax
from jax.experimental import pallas as pl
from jax.experimental.pallas import tpu as pltpu
from jax.sharding import PartitionSpec as P

N = 16
DH = 128
GROUPS = 4
MEMBERS = 8
EPS = 1e-06
UNROLL = 4
MESH = pl.DeviceIdType.MESH
F32 = jnp.float32
BF16 = jnp.bfloat16


def dot(a, b, ca, cb):
    return lax.dot_general(a, b, (((ca,), (cb,)), ((), ())), preferred_element_type=F32)


def kernel(
    q_hbm, k_hbm, v_hbm, g_hbm,
    n_hbm, qg_hbm, kg_hbm, vg_hbm,
    q_v, k_v, v_v, g_v,
    kv_s, kv_r, a_s, a_r, q_r, g_r,
    p_s, p_r, t_s, t_r,
    sc_v, al_v, sg_v, kl_v, vl_v,
    n_v, qg_v, kg_v, vg_v,
    za, zb, zc, zd, ze,
    in_sem, out_sem, self_sem, send_sem, recv_sem, zsend_sem, z1_sem, z2_sem, z3_sem,
):
    me = lax.axis_index("head")
    seq = lax.axis_index("seq")
    group = seq // MEMBERS
    member = seq % MEMBERS

    def plane(i):
        return (i, seq)

    def column(m):
        return (me, group * MEMBERS + m)

    def across(g):
        return (me, g * MEMBERS + member)

    def turn(j):
        return lax.rem(me + j, N)

    def cols(h):
        return pl.ds(pl.multiple_of(h * DH, DH), DH)

    barrier = pltpu.get_barrier_semaphore()
    loads = [
        pltpu.make_async_copy(src, dst, in_sem.at[i])
        for i, (src, dst) in enumerate(((k_hbm, k_v), (v_hbm, v_v), (q_hbm, q_v), (g_hbm, g_v)))
    ]
    for load in loads:
        load.start()

    @pl.loop(1, N)
    def _(j):
        pl.semaphore_signal(barrier, inc=1, device_id=plane(turn(j)), device_id_type=MESH)

    for j in range(1, MEMBERS):
        pl.semaphore_signal(
            barrier, inc=1, device_id=column(lax.rem(member + j, MEMBERS)), device_id_type=MESH
        )
    for j in range(1, GROUPS):
        pl.semaphore_signal(
            barrier, inc=1, device_id=across(lax.rem(group + j, GROUPS)), device_id_type=MESH
        )

    def send(which, src, dst, to):
        return pltpu.make_async_remote_copy(
            src_ref=src,
            dst_ref=dst,
            send_sem=send_sem.at[which],
            recv_sem=recv_sem.at[which, me],
            device_id=plane(to),
            device_id_type=MESH,
        )

    def arrived(which, buf, src):
        pltpu.make_async_remote_copy(
            src_ref=buf.at[src],
            dst_ref=buf.at[src],
            send_sem=send_sem.at[which],
            recv_sem=recv_sem.at[which, src],
            device_id=plane(me),
            device_id_type=MESH,
        ).wait_recv()

    def all_sent(which, buf):
        pltpu.make_async_copy(
            buf.at[pl.ds(0, N - 1)], buf.at[pl.ds(0, N - 1)], send_sem.at[which]
        ).wait()

    loads[0].wait()
    loads[1].wait()

    @pl.loop(0, N // UNROLL)
    def _(t):
        for u in range(UNROLL):
            h = turn(t * UNROLL + u + 1)
            kv_s[h] = dot(k_v[:, cols(h)], v_v[:, cols(h)], 0, 0).astype(BF16)

    kv_r[me] = kv_s[me]
    pl.semaphore_wait(barrier, N - 1 + MEMBERS - 1 + GROUPS - 1)

    @pl.loop(1, N)
    def _(j):
        h = turn(j)
        send(0, kv_s.at[h], kv_r.at[me], h).start()

    loads[2].wait()
    loads[3].wait()
    mine_q = pltpu.make_async_copy(q_v.at[:, cols(me)], q_r.at[me], self_sem.at[0])
    mine_g = pltpu.make_async_copy(g_v.at[:, cols(me)], g_r.at[me], self_sem.at[1])
    mine_q.start()
    mine_g.start()

    @pl.loop(1, N)
    def _(j):
        h = turn(j)
        send(1, q_v.at[:, cols(h)], q_r.at[me], h).start()
        send(2, g_v.at[:, cols(h)], g_r.at[me], h).start()

    rows = lax.broadcasted_iota(jnp.int32, (DH, DH), 0)
    causal = rows >= lax.broadcasted_iota(jnp.int32, (DH, DH), 1)

    @pl.loop(0, N // UNROLL)
    def _(t):
        for u in range(UNROLL):
            h = turn(t * UNROLL + u + 1)
            scores = dot(q_v[:, cols(h)], k_v[:, cols(h)], 1, 1)
            scores = jnp.where(causal, scores, F32(0.0)).astype(BF16)
            sc_v[h] = scores
            local = dot(scores, v_v[:, cols(h)], 1, 0)
            al_v[h] = local
            a_s[h] = local.astype(BF16)

        for u in range(UNROLL):
            j = t * UNROLL + u + 1
            h = turn(j)

            @pl.when(j < N)
            def _():
                send(3, a_s.at[h], a_r.at[me], h).start()

    a_r[me] = a_s[me]

    def exchange(first, reverse, totals):
        z = 1 if reverse else 0

        def zsend(step, src, dst, sem, to):
            return pltpu.make_async_remote_copy(
                src_ref=src,
                dst_ref=dst,
                send_sem=zsend_sem.at[z, step],
                recv_sem=sem,
                device_id=to,
                device_id_type=MESH,
            )

        def zwait(dst, sem):
            pltpu.make_async_copy(dst, dst, sem).wait()

        za[z] = totals.reshape(MEMBERS, DH // MEMBERS, DH)
        for j in range(1, MEMBERS):
            m = lax.rem(member + j, MEMBERS)
            zsend(0, za.at[z, m], zb.at[z, member], z1_sem.at[z, member], column(m)).start()
        zb[z, member] = za[z, member]
        first()
        for j in range(1, MEMBERS):
            m = lax.rem(member + j, MEMBERS)
            zwait(zb.at[z, m], z1_sem.at[z, m])
        total = zb[z, 0]
        for m in range(1, MEMBERS):
            total += zb[z, m]
        zc[z, GROUPS] = total
        zc[z, group] = jnp.zeros_like(total)
        for j in range(1, GROUPS):
            g = lax.rem(group + j, GROUPS)
            zsend(1, zc.at[z, GROUPS], zc.at[z, group], z2_sem.at[z, group], across(g)).start()
        for j in range(1, GROUPS):
            g = lax.rem(group + j, GROUPS)
            zwait(zc.at[z, g], z2_sem.at[z, g])
        running = jnp.zeros_like(total)
        for g in range(GROUPS):
            counts = (g > group) if reverse else (g < group)
            running += jnp.where(counts, zc[z, g], F32(0.0))
        for m in range(MEMBERS):
            m = MEMBERS - 1 - m if reverse else m
            zd[z, m] = running
            running += zb[z, m]
        for j in range(1, MEMBERS):
            m = lax.rem(member + j, MEMBERS)
            zsend(2, zd.at[z, m], ze.at[z, member], z3_sem.at[z, member], column(m)).start()
        ze[z, member] = zd[z, member]
        for j in range(1, MEMBERS):
            m = lax.rem(member + j, MEMBERS)
            zwait(ze.at[z, m], z3_sem.at[z, m])
        return ze[z].reshape(DH, DH)

    def exchange_sent(z):
        pltpu.make_async_copy(
            za.at[z, pl.ds(0, MEMBERS - 1)], za.at[z, pl.ds(0, MEMBERS - 1)], zsend_sem.at[z, 0]
        ).wait()
        pltpu.make_async_copy(
            zc.at[z, pl.ds(0, GROUPS - 1)], zc.at[z, pl.ds(0, GROUPS - 1)], zsend_sem.at[z, 1]
        ).wait()
        pltpu.make_async_copy(
            zd.at[z, pl.ds(0, MEMBERS - 1)], zd.at[z, pl.ds(0, MEMBERS - 1)], zsend_sem.at[z, 2]
        ).wait()

    @pl.loop(1, N)
    def _(j):
        arrived(0, kv_r, turn(j))

    total = kv_r[0].astype(F32)
    for i in range(1, N):
        total += kv_r[i].astype(F32)
    state = exchange(lambda: None, False, total)
    for i in range(N):
        p_s[i] = state.astype(BF16)
        state += kv_r[i].astype(F32)
    p_r[me] = p_s[me]

    mine_q.wait()
    mine_g.wait()

    @pl.loop(1, N)
    def _(j):
        i = turn(j)
        arrived(1, q_r, i)
        arrived(2, g_r, i)
        arrived(3, a_r, i)

    def normalize(attn, cot):
        inv_rms = lax.rsqrt(jnp.mean(attn * attn, axis=-1, keepdims=True) + EPS)
        normed = attn * inv_rms
        cot = cot.astype(F32)
        along = jnp.mean(cot * normed, axis=-1, keepdims=True)
        return normed, (inv_rms * (cot - normed * along)).astype(BF16)

    @pl.loop(0, N // UNROLL)
    def _(t):
        for u in range(UNROLL):
            i = t * UNROLL + u
            q = q_r[i]
            attn = a_r[i].astype(F32) + dot(q, p_s[i], 1, 0)
            _, out_grad = normalize(attn, g_r[i])
            sg_v[i] = dot(q, out_grad, 0, 0)

    total = sg_v[0]
    for i in range(1, N):
        total += sg_v[i]

    def send_states():
        @pl.loop(1, N)
        def _(j):
            i = turn(j)
            send(4, p_s.at[i], p_r.at[me], i).start()

    later = exchange(send_states, True, total)
    for i in range(N - 1, -1, -1):
        t_s[i] = later.astype(BF16)
        later += sg_v[i]
    t_r[me] = t_s[me]

    @pl.loop(1, N)
    def _(j):
        i = turn(j)
        send(5, t_s.at[i], t_r.at[me], i).start()

    @pl.loop(1, N)
    def _(j):
        arrived(4, p_r, turn(j))

    @pl.loop(0, N // UNROLL)
    def _(t):
        for u in range(UNROLL):
            h = t * UNROLL + u
            c = cols(h)
            q = q_v[:, c]
            state = p_r[h]
            attn = al_v[h] + dot(q, state, 1, 0)
            normed, out_grad = normalize(attn, g_v[:, c])
            n_v[:, c] = normed.astype(BF16)
            grads = dot(out_grad, v_v[:, c], 1, 1)
            grads = jnp.where(causal, grads, F32(0.0)).astype(BF16)
            query_grad = dot(grads, k_v[:, c], 1, 0) + dot(out_grad, state, 1, 1)
            qg_v[:, c] = query_grad.astype(BF16)
            kl_v[h] = dot(grads, q, 0, 0)
            vl_v[h] = dot(sc_v[h], out_grad, 0, 0)

    stores = [
        pltpu.make_async_copy(src, dst, out_sem.at[i])
        for i, (src, dst) in enumerate(
            ((n_v, n_hbm), (qg_v, qg_hbm), (kg_v, kg_hbm), (vg_v, vg_hbm))
        )
    ]
    stores[0].start()
    stores[1].start()

    @pl.loop(1, N)
    def _(j):
        arrived(5, t_r, turn(j))

    @pl.loop(0, N // UNROLL)
    def _(t):
        for u in range(UNROLL):
            h = t * UNROLL + u
            c = cols(h)
            grad_state = t_r[h]
            kg_v[:, c] = (kl_v[h] + dot(v_v[:, c], grad_state, 1, 1)).astype(BF16)
            vg_v[:, c] = (vl_v[h] + dot(k_v[:, c], grad_state, 1, 0)).astype(BF16)

    stores[2].start()
    stores[3].start()
    for which, buf in enumerate((kv_s, q_r, g_r, a_s, p_s, t_s)):
        all_sent(which, buf)
    exchange_sent(0)
    exchange_sent(1)
    for store in stores:
        store.wait()


def shards(q, k, v, g):
    tokens, width = q.shape
    wide = pltpu.VMEM((tokens, width), BF16)
    blocks = pltpu.VMEM((N, DH, DH), BF16)
    sums = pltpu.VMEM((N, DH, DH), F32)
    eighths = pltpu.VMEM((2, MEMBERS, DH // MEMBERS, DH), F32)
    groups = pltpu.VMEM((2, GROUPS + 1, DH // MEMBERS, DH), F32)
    dma = pltpu.SemaphoreType.DMA
    return pl.pallas_call(
        kernel,
        out_shape=[jax.ShapeDtypeStruct((tokens, width), BF16)] * 4,
        in_specs=[pl.BlockSpec(memory_space=pl.ANY)] * 4,
        out_specs=[pl.BlockSpec(memory_space=pl.ANY)] * 4,
        scratch_shapes=[wide] * 4
        + [blocks] * 10
        + [blocks] + [sums] * 4
        + [wide] * 4
        + [eighths, eighths, groups, eighths, eighths]
        + [dma((4,)), dma((4,)), dma((2,)), dma((6,)), dma((6, N))]
        + [dma((2, 3)), dma((2, MEMBERS)), dma((2, GROUPS)), dma((2, MEMBERS))],
        compiler_params=pltpu.CompilerParams(
            collective_id=0, has_side_effects=True, vmem_limit_bytes=60 * 1024 * 1024
        ),
        cost_estimate=pl.CostEstimate(
            flops=2 * 14 * N * DH**3, bytes_accessed=16 * tokens * width, transcendentals=0
        ),
    )(q, k, v, g)


def solution(mesh):
    spec = P(("seq", "head"), None)
    return jax.shard_map(
        shards, mesh=mesh, in_specs=(spec,) * 4, out_specs=(spec,) * 4, check_vma=False
    )
```

```python
import jax
import jax.numpy as jnp
from jax import lax
from jax.experimental import pallas as pl
from jax.experimental.pallas import tpu as pltpu
from jax.sharding import PartitionSpec as P

N = 16
DH = 128
GROUPS = 4
MEMBERS = 8
EPS = 1e-06
STEPS = (
    (2, 2), (2, 1), (1, 2), (2, 3), (3, 2), (1, 1), (3, 3), (1, 3), (3, 1),
    (2, 0), (0, 2), (1, 0), (0, 1), (3, 0), (0, 3),
)
EARLY = 0
MESH = pl.DeviceIdType.MESH
F32 = jnp.float32
BF16 = jnp.bfloat16


def dot(a, b, ca, cb):
    return lax.dot_general(a, b, (((ca,), (cb,)), ((), ())), preferred_element_type=F32)


def kernel(
    q_hbm, k_hbm, v_hbm, g_hbm,
    n_hbm, qg_hbm, t_hbm, kl_hbm, vl_hbm,
    q_v, k_v, v_v, g_v,
    kv_s, kv_r, a_s, a_r, q_r, g_r,
    p_s, p_r, t_s,
    sc_v, al_v, sg_v, kl_v, vl_v,
    n_v, qg_v,
    za, zb, zc, zd, ze,
    in_sem, out_sem, self_sem, send_sem, recv_sem, zsend_sem, z1_sem, z2_sem, z3_sem,
):
    me = lax.axis_index("head")
    seq = lax.axis_index("seq")
    group = seq // MEMBERS
    member = seq % MEMBERS

    def plane(i):
        return (i, seq)

    def column(m):
        return (me, group * MEMBERS + m)

    def across(g):
        return (me, g * MEMBERS + member)

    def turn(j):
        return lax.rem(me + j, N)

    def cols(h):
        if isinstance(h, int):
            return pl.ds(h * DH, DH)
        return pl.ds(pl.multiple_of(h * DH, DH), DH)

    y, x = me // 4, me % 4
    others = [lax.rem(y + dy, 4) * 4 + lax.rem(x + dx, 4) for dx, dy in STEPS]

    barrier = pltpu.get_barrier_semaphore()
    loads = [
        pltpu.make_async_copy(src, dst, in_sem.at[i])
        for i, (src, dst) in enumerate(((k_hbm, k_v), (v_hbm, v_v), (q_hbm, q_v), (g_hbm, g_v)))
    ]
    for load in loads:
        load.start()

    @pl.loop(1, N)
    def _(j):
        pl.semaphore_signal(barrier, inc=1, device_id=plane(turn(j)), device_id_type=MESH)

    for j in range(1, MEMBERS):
        pl.semaphore_signal(
            barrier, inc=1, device_id=column(lax.rem(member + j, MEMBERS)), device_id_type=MESH
        )
    for j in range(1, GROUPS):
        pl.semaphore_signal(
            barrier, inc=1, device_id=across(lax.rem(group + j, GROUPS)), device_id_type=MESH
        )

    def send(which, src, dst, to):
        return pltpu.make_async_remote_copy(
            src_ref=src,
            dst_ref=dst,
            send_sem=send_sem.at[which],
            recv_sem=recv_sem.at[which, me],
            device_id=plane(to),
            device_id_type=MESH,
        )

    def arrived(which, buf, src):
        pltpu.make_async_remote_copy(
            src_ref=buf.at[src],
            dst_ref=buf.at[src],
            send_sem=send_sem.at[which],
            recv_sem=recv_sem.at[which, src],
            device_id=plane(me),
            device_id_type=MESH,
        ).wait_recv()

    def all_sent(which, buf):
        pltpu.make_async_copy(
            buf.at[pl.ds(0, N - 1)], buf.at[pl.ds(0, N - 1)], send_sem.at[which]
        ).wait()

    loads[0].wait()
    loads[1].wait()

    for h in range(N):
        kv_s[h] = dot(k_v[:, cols(h)], v_v[:, cols(h)], 0, 0).astype(BF16)

    kv_r[me] = kv_s[me]
    pl.semaphore_wait(barrier, N - 1 + MEMBERS - 1 + GROUPS - 1)

    for h in others:
        send(0, kv_s.at[h], kv_r.at[me], h).start()

    loads[2].wait()
    loads[3].wait()
    mine_q = pltpu.make_async_copy(q_v.at[:, cols(me)], q_r.at[me], self_sem.at[0])
    mine_g = pltpu.make_async_copy(g_v.at[:, cols(me)], g_r.at[me], self_sem.at[1])
    mine_q.start()
    mine_g.start()

    for h in others:
        send(1, q_v.at[:, cols(h)], q_r.at[me], h).start()
    for h in others:
        send(2, g_v.at[:, cols(h)], g_r.at[me], h).start()

    rows = lax.broadcasted_iota(jnp.int32, (DH, DH), 0)
    causal = rows >= lax.broadcasted_iota(jnp.int32, (DH, DH), 1)

    for h in range(N):
        scores = dot(q_v[:, cols(h)], k_v[:, cols(h)], 1, 1)
        scores = jnp.where(causal, scores, F32(0.0)).astype(BF16)
        sc_v[h] = scores
        local = dot(scores, v_v[:, cols(h)], 1, 0)
        al_v[h] = local
        a_s[h] = local.astype(BF16)
    for h in others:
        send(3, a_s.at[h], a_r.at[me], h).start()
    a_r[me] = a_s[me]

    def exchange(reverse, totals, first, second):
        z = 1 if reverse else 0

        def zsend(step, src, dst, sem, to):
            return pltpu.make_async_remote_copy(
                src_ref=src,
                dst_ref=dst,
                send_sem=zsend_sem.at[z, step],
                recv_sem=sem,
                device_id=to,
                device_id_type=MESH,
            )

        def zwait(dst, sem):
            pltpu.make_async_copy(dst, dst, sem).wait()

        za[z] = totals.reshape(MEMBERS, DH // MEMBERS, DH)
        for j in range(1, MEMBERS):
            m = lax.rem(member + j, MEMBERS)
            zsend(0, za.at[z, m], zb.at[z, member], z1_sem.at[z, member], column(m)).start()
        zb[z, member] = za[z, member]
        first()
        for j in range(1, MEMBERS):
            m = lax.rem(member + j, MEMBERS)
            zwait(zb.at[z, m], z1_sem.at[z, m])
        total = zb[z, 0]
        for m in range(1, MEMBERS):
            total += zb[z, m]
        zc[z, GROUPS] = total
        zc[z, group] = jnp.zeros_like(total)
        for j in range(1, GROUPS):
            g = lax.rem(group + j, GROUPS)
            zsend(1, zc.at[z, GROUPS], zc.at[z, group], z2_sem.at[z, group], across(g)).start()
        second()
        for j in range(1, GROUPS):
            g = lax.rem(group + j, GROUPS)
            zwait(zc.at[z, g], z2_sem.at[z, g])
        running = jnp.zeros_like(total)
        for g in range(GROUPS):
            counts = (g > group) if reverse else (g < group)
            running += jnp.where(counts, zc[z, g], F32(0.0))
        for m in range(MEMBERS):
            m = MEMBERS - 1 - m if reverse else m
            zd[z, m] = running
            running += zb[z, m]
        for j in range(1, MEMBERS):
            m = lax.rem(member + j, MEMBERS)
            zsend(2, zd.at[z, m], ze.at[z, member], z3_sem.at[z, member], column(m)).start()
        ze[z, member] = zd[z, member]
        for j in range(1, MEMBERS):
            m = lax.rem(member + j, MEMBERS)
            zwait(ze.at[z, m], z3_sem.at[z, m])
        return ze[z].reshape(DH, DH)

    def exchange_sent(z):
        pltpu.make_async_copy(
            za.at[z, pl.ds(0, MEMBERS - 1)], za.at[z, pl.ds(0, MEMBERS - 1)], zsend_sem.at[z, 0]
        ).wait()
        pltpu.make_async_copy(
            zc.at[z, pl.ds(0, GROUPS - 1)], zc.at[z, pl.ds(0, GROUPS - 1)], zsend_sem.at[z, 1]
        ).wait()
        pltpu.make_async_copy(
            zd.at[z, pl.ds(0, MEMBERS - 1)], zd.at[z, pl.ds(0, MEMBERS - 1)], zsend_sem.at[z, 2]
        ).wait()

    @pl.loop(1, N)
    def _(j):
        arrived(0, kv_r, turn(j))

    total = kv_r[0].astype(F32)
    for i in range(1, N):
        total += kv_r[i].astype(F32)
    state = exchange(False, total, lambda: None, lambda: None)
    for i in range(N):
        p_s[i] = state.astype(BF16)
        state += kv_r[i].astype(F32)
    p_r[me] = p_s[me]

    mine_q.wait()
    mine_g.wait()

    @pl.loop(1, N)
    def _(j):
        i = turn(j)
        arrived(1, q_r, i)
        arrived(2, g_r, i)
        arrived(3, a_r, i)

    def normalize(attn, cot):
        inv_rms = lax.rsqrt(jnp.mean(attn * attn, axis=-1, keepdims=True) + EPS)
        normed = attn * inv_rms
        cot = cot.astype(F32)
        along = jnp.mean(cot * normed, axis=-1, keepdims=True)
        return normed, (inv_rms * (cot - normed * along)).astype(BF16)

    for i in range(N):
        q = q_r[i]
        attn = a_r[i].astype(F32) + dot(q, p_s[i], 1, 0)
        _, out_grad = normalize(attn, g_r[i])
        sg_v[i] = dot(q, out_grad, 0, 0)

    total = sg_v[0]
    for i in range(1, N):
        total += sg_v[i]

    def send_states():
        for i in others:
            send(4, p_s.at[i], p_r.at[me], i).start()

    def home(heads):
        for h in heads:
            c = cols(h)
            q = q_v[:, c]
            state = p_r[h]
            attn = al_v[h] + dot(q, state, 1, 0)
            normed, out_grad = normalize(attn, g_v[:, c])
            n_v[:, c] = normed.astype(BF16)
            grads = dot(out_grad, v_v[:, c], 1, 1)
            grads = jnp.where(causal, grads, F32(0.0)).astype(BF16)
            query_grad = dot(grads, k_v[:, c], 1, 0) + dot(out_grad, state, 1, 1)
            qg_v[:, c] = query_grad.astype(BF16)
            kl_v[h] = dot(grads, q, 0, 0)
            vl_v[h] = dot(sc_v[h], out_grad, 0, 0)

    def early():
        @pl.loop(1, N)
        def _(j):
            arrived(4, p_r, turn(j))

        home(range(EARLY))

    later = exchange(True, total, send_states, early)
    for i in range(N - 1, -1, -1):
        t_s[i] = later.astype(BF16)
        later += sg_v[i]
    for i in others:
        send(5, t_s.at[i], t_hbm.at[me], i).start()
    mine_t = pltpu.make_async_copy(t_s.at[me], t_hbm.at[me], self_sem.at[2])
    mine_t.start()
    home(range(EARLY, N))

    stores = [
        pltpu.make_async_copy(src, dst, out_sem.at[i])
        for i, (src, dst) in enumerate(
            ((n_v, n_hbm), (qg_v, qg_hbm), (kl_v, kl_hbm), (vl_v, vl_hbm))
        )
    ]
    for store in stores:
        store.start()

    @pl.loop(1, N)
    def _(j):
        arrived(5, t_hbm, turn(j))

    mine_t.wait()
    for which, buf in enumerate((kv_s, q_r, g_r, a_s, p_s, t_s)):
        all_sent(which, buf)
    exchange_sent(0)
    exchange_sent(1)
    for store in stores:
        store.wait()


def finish(
    n_hbm, qg_hbm, t_hbm, kl_hbm, vl_hbm, k_hbm, v_hbm,
    n_out, qg_out, kg_out, vg_out,
    t_v, kl_v, vl_v, k_v, v_v, kg_v, vg_v, n_v, qg_v,
    in_sem, out_sem, pass_sem,
):
    half = N // 2
    loads = []
    for p in range(2):
        heads, wide = pl.ds(p * half, half), pl.ds(p * half * DH, half * DH)
        pairs = (
            (t_hbm.at[heads], t_v.at[heads]),
            (v_hbm.at[:, wide], v_v.at[:, wide]),
            (k_hbm.at[:, wide], k_v.at[:, wide]),
            (kl_hbm.at[heads], kl_v.at[heads]),
            (vl_hbm.at[heads], vl_v.at[heads]),
        )
        loads.append(
            [pltpu.make_async_copy(a, b, in_sem.at[p, i]) for i, (a, b) in enumerate(pairs)]
        )
    passes = [
        pltpu.make_async_copy(n_hbm, n_v, pass_sem.at[0]),
        pltpu.make_async_copy(qg_hbm, qg_v, pass_sem.at[1]),
    ]
    for load in loads[0] + loads[1] + passes:
        load.start()
    stores = [
        pltpu.make_async_copy(n_v, n_out, pass_sem.at[2]),
        pltpu.make_async_copy(qg_v, qg_out, pass_sem.at[3]),
    ]
    for p in range(2):
        for load in loads[p]:
            load.wait()
        for h in range(p * half, (p + 1) * half):
            c = pl.ds(h * DH, DH)
            kg_v[:, c] = (kl_v[h] + dot(v_v[:, c], t_v[h], 1, 1)).astype(BF16)
            vg_v[:, c] = (vl_v[h] + dot(k_v[:, c], t_v[h], 1, 0)).astype(BF16)
        wide = pl.ds(p * half * DH, half * DH)
        for i, (src, dst) in enumerate(((kg_v, kg_out), (vg_v, vg_out))):
            stores.append(
                pltpu.make_async_copy(src.at[:, wide], dst.at[:, wide], out_sem.at[p, i])
            )
            stores[-1].start()
        passes[p].wait()
        stores[p].start()
    for store in stores:
        store.wait()


def shards(q, k, v, g):
    tokens, width = q.shape
    wide = pltpu.VMEM((tokens, width), BF16)
    blocks = pltpu.VMEM((N, DH, DH), BF16)
    sums = pltpu.VMEM((N, DH, DH), F32)
    eighths = pltpu.VMEM((2, MEMBERS, DH // MEMBERS, DH), F32)
    groups = pltpu.VMEM((2, GROUPS + 1, DH // MEMBERS, DH), F32)
    dma = pltpu.SemaphoreType.DMA
    whole = jax.ShapeDtypeStruct((tokens, width), BF16)
    states = jax.ShapeDtypeStruct((N, DH, DH), BF16)
    parts = jax.ShapeDtypeStruct((N, DH, DH), F32)
    anywhere = pl.BlockSpec(memory_space=pl.ANY)
    normed, query_grad, later, key_part, value_part = pl.pallas_call(
        kernel,
        out_shape=[whole, whole, states, parts, parts],
        in_specs=[anywhere] * 4,
        out_specs=[anywhere] * 5,
        scratch_shapes=[wide] * 4
        + [blocks] * 9
        + [blocks] + [sums] * 4
        + [wide] * 2
        + [eighths, eighths, groups, eighths, eighths]
        + [dma((4,)), dma((4,)), dma((3,)), dma((6,)), dma((6, N))]
        + [dma((2, 3)), dma((2, MEMBERS)), dma((2, GROUPS)), dma((2, MEMBERS))],
        compiler_params=pltpu.CompilerParams(
            collective_id=0, has_side_effects=True, vmem_limit_bytes=60 * 1024 * 1024
        ),
        cost_estimate=pl.CostEstimate(
            flops=2 * 12 * N * DH**3, bytes_accessed=16 * tokens * width, transcendentals=0
        ),
    )(q, k, v, g)
    return pl.pallas_call(
        finish,
        out_shape=[whole] * 4,
        in_specs=[anywhere] * 7,
        out_specs=[anywhere] * 4,
        scratch_shapes=[blocks, sums, sums]
        + [wide] * 6
        + [dma((2, 5)), dma((2, 2)), dma((4,))],
        compiler_params=pltpu.CompilerParams(vmem_limit_bytes=60 * 1024 * 1024),
        cost_estimate=pl.CostEstimate(
            flops=2 * 2 * N * DH**3, bytes_accessed=18 * tokens * width, transcendentals=0
        ),
    )(normed, query_grad, later, key_part, value_part, k, v)


def solution(mesh):
    spec = P(("seq", "head"), None)
    return jax.shard_map(
        shards, mesh=mesh, in_specs=(spec,) * 4, out_specs=(spec,) * 4, check_vma=False
    )
```

```python
import jax
import jax.numpy as jnp
from jax import lax
from jax.experimental import pallas as pl
from jax.experimental.pallas import tpu as pltpu
from jax.sharding import PartitionSpec as P

N = 16
DH = 128
PARTS = 2
GROUPS = 4
MEMBERS = 8
EPS = 1e-06
STEPS = (
    (2, 2), (2, 1), (1, 2), (2, 3), (3, 2), (1, 1), (3, 3), (1, 3), (3, 1),
    (2, 0), (0, 2), (1, 0), (0, 1), (3, 0), (0, 3),
)
MESH = pl.DeviceIdType.MESH
F32 = jnp.float32
BF16 = jnp.bfloat16


def dot(a, b, ca, cb):
    return lax.dot_general(a, b, (((ca,), (cb,)), ((), ())), preferred_element_type=F32)


def kernel(
    q_hbm, k_hbm, v_hbm, g_hbm,
    n_hbm, qg_hbm, t_hbm, kl_hbm, vl_hbm,
    q_v, k_v, v_v, g_v,
    kv_s, kv_r, a_s, a_r, q_r, g_r,
    p_s, p_r, t_s,
    sc_v, al_v, sg_v, kl_v, vl_v,
    n_v, qg_v,
    za, zb, zc, zd, ze,
    in_sem, out_sem, self_sem, send_sem, recv_sem,
    zsend_sem, zacross_sem, z1_sem, z2_sem, z3_sem, ready_sem,
):
    me = lax.axis_index("head")
    seq = lax.axis_index("seq")
    group = seq // MEMBERS
    member = seq % MEMBERS

    def plane(i):
        return (i, seq)

    def column(m):
        return (me, group * MEMBERS + m)

    def across(g):
        return (me, g * MEMBERS + member)

    def turn(j):
        return lax.rem(me + j, N)

    def cols(h):
        if isinstance(h, int):
            return pl.ds(h * DH, DH)
        return pl.ds(pl.multiple_of(h * DH, DH), DH)

    y, x = me // 4, me % 4
    others = [lax.rem(y + dy, 4) * 4 + lax.rem(x + dx, 4) for dx, dy in STEPS]

    def peers(reverse):
        for j in range(1, GROUPS):
            g = lax.rem(group + j, GROUPS)
            yield (g, g < group, g > group) if reverse else (g, g > group, g < group)

    barrier = pltpu.get_barrier_semaphore()
    loads = [
        pltpu.make_async_copy(src, dst, in_sem.at[i])
        for i, (src, dst) in enumerate(((k_hbm, k_v), (v_hbm, v_v), (q_hbm, q_v), (g_hbm, g_v)))
    ]
    loads[0].start()
    loads[1].start()
    for i in others:
        pl.semaphore_signal(barrier, inc=1, device_id=plane(i), device_id_type=MESH)
    for g, above, _ in peers(False):

        @pl.when(above)
        def _():
            pl.semaphore_signal(barrier, inc=1, device_id=across(g), device_id_type=MESH)

    for j in range(1, MEMBERS):
        pl.semaphore_signal(
            barrier, inc=1, device_id=column(lax.rem(member + j, MEMBERS)), device_id_type=MESH
        )
    loads[2].start()
    loads[3].start()

    def send(which, src, dst, to):
        return pltpu.make_async_remote_copy(
            src_ref=src,
            dst_ref=dst,
            send_sem=send_sem.at[which],
            recv_sem=recv_sem.at[which, me],
            device_id=plane(to),
            device_id_type=MESH,
        )

    def arrived(which, buf, src):
        pltpu.make_async_remote_copy(
            src_ref=buf.at[src],
            dst_ref=buf.at[src],
            send_sem=send_sem.at[which],
            recv_sem=recv_sem.at[which, src],
            device_id=plane(me),
            device_id_type=MESH,
        ).wait_recv()

    def all_sent(which, buf):
        pltpu.make_async_copy(
            buf.at[pl.ds(0, N - 1)], buf.at[pl.ds(0, N - 1)], send_sem.at[which]
        ).wait()

    loads[0].wait()
    loads[1].wait()

    for h in range(N):
        kv_s[h] = dot(k_v[:, cols(h)], v_v[:, cols(h)], 0, 0).astype(BF16)

    kv_r[me] = kv_s[me]
    pl.semaphore_wait(barrier, N - 1 + MEMBERS - 1 + group)
    for g, _, below in peers(False):

        @pl.when(below)
        def _():
            pl.semaphore_signal(ready_sem.at[group], inc=1, device_id=across(g), device_id_type=MESH)


    for h in others:
        send(0, kv_s.at[h], kv_r.at[me], h).start()

    loads[2].wait()
    loads[3].wait()
    mine_q = pltpu.make_async_copy(q_v.at[:, cols(me)], q_r.at[me], self_sem.at[0])
    mine_g = pltpu.make_async_copy(g_v.at[:, cols(me)], g_r.at[me], self_sem.at[1])
    mine_q.start()
    mine_g.start()

    for h in others:
        send(1, q_v.at[:, cols(h)], q_r.at[me], h).start()
    for h in others:
        send(2, g_v.at[:, cols(h)], g_r.at[me], h).start()

    rows = lax.broadcasted_iota(jnp.int32, (DH, DH), 0)
    causal = rows >= lax.broadcasted_iota(jnp.int32, (DH, DH), 1)

    for h in range(N):
        scores = dot(q_v[:, cols(h)], k_v[:, cols(h)], 1, 1)
        scores = jnp.where(causal, scores, F32(0.0)).astype(BF16)
        sc_v[h] = scores
        local = dot(scores, v_v[:, cols(h)], 1, 0)
        al_v[h] = local
        a_s[h] = local.astype(BF16)
    a_r[me] = a_s[me]

    def across_copy(z, g):
        return pltpu.make_async_remote_copy(
            src_ref=zc.at[z, GROUPS],
            dst_ref=zc.at[z, group],
            send_sem=zacross_sem.at[z, g],
            recv_sem=z2_sem.at[z, group],
            device_id=across(g),
            device_id_type=MESH,
        )

    def exchange(reverse, totals, first, second):
        z = 1 if reverse else 0

        def zsend(step, src, dst, sem, to):
            return pltpu.make_async_remote_copy(
                src_ref=src,
                dst_ref=dst,
                send_sem=zsend_sem.at[z, step],
                recv_sem=sem,
                device_id=to,
                device_id_type=MESH,
            )

        def zwait(dst, sem):
            pltpu.make_async_copy(dst, dst, sem).wait()

        za[z] = totals.reshape(MEMBERS, DH // MEMBERS, DH)
        for j in range(1, MEMBERS):
            m = lax.rem(member + j, MEMBERS)
            zsend(0, za.at[z, m], zb.at[z, member], z1_sem.at[z, member], column(m)).start()
        zb[z, member] = za[z, member]
        first()
        for j in range(1, MEMBERS):
            m = lax.rem(member + j, MEMBERS)
            zwait(zb.at[z, m], z1_sem.at[z, m])
        total = zb[z, 0]
        for m in range(1, MEMBERS):
            total += zb[z, m]
        zc[z, GROUPS] = total
        zc[z, group] = jnp.zeros_like(total)
        for g, wanted, _ in peers(reverse):

            @pl.when(wanted)
            def _():
                if not reverse:
                    pl.semaphore_wait(ready_sem.at[g], 1)
                across_copy(z, g).start()

        second()
        for g, _, given in peers(reverse):

            @pl.when(given)
            def _():
                zwait(zc.at[z, g], z2_sem.at[z, g])

            @pl.when(jnp.logical_not(given))
            def _():
                zc[z, g] = jnp.zeros_like(total)

        running = zc[z, 0]
        for g in range(1, GROUPS):
            running += zc[z, g]
        for m in range(MEMBERS):
            m = MEMBERS - 1 - m if reverse else m
            zd[z, m] = running
            running += zb[z, m]
        for j in range(1, MEMBERS):
            m = lax.rem(member + j, MEMBERS)
            zsend(2, zd.at[z, m], ze.at[z, member], z3_sem.at[z, member], column(m)).start()
        ze[z, member] = zd[z, member]
        for j in range(1, MEMBERS):
            m = lax.rem(member + j, MEMBERS)
            zwait(ze.at[z, m], z3_sem.at[z, m])
        return ze[z].reshape(DH, DH)

    def exchange_sent(z):
        pltpu.make_async_copy(
            za.at[z, pl.ds(0, MEMBERS - 1)], za.at[z, pl.ds(0, MEMBERS - 1)], zsend_sem.at[z, 0]
        ).wait()
        for g, wanted, _ in peers(z == 1):

            @pl.when(wanted)
            def _():
                across_copy(z, g).wait_send()

        pltpu.make_async_copy(
            zd.at[z, pl.ds(0, MEMBERS - 1)], zd.at[z, pl.ds(0, MEMBERS - 1)], zsend_sem.at[z, 2]
        ).wait()

    @pl.loop(1, N)
    def _(j):
        arrived(0, kv_r, turn(j))

    total = kv_r[0].astype(F32)
    for i in range(1, N):
        total += kv_r[i].astype(F32)
    def send_rest():
        for h in others:
            send(3, a_s.at[h], a_r.at[me], h).start()

    state = exchange(False, total, send_rest, lambda: None)
    for i in range(N):
        p_s[i] = state.astype(BF16)
        state += kv_r[i].astype(F32)
    p_r[me] = p_s[me]

    mine_q.wait()
    mine_g.wait()

    @pl.loop(1, N)
    def _(j):
        i = turn(j)
        arrived(1, q_r, i)
        arrived(2, g_r, i)
        arrived(3, a_r, i)

    def normalize(attn, cot):
        inv_rms = lax.rsqrt(jnp.mean(attn * attn, axis=-1, keepdims=True) + EPS)
        normed = attn * inv_rms
        cot = cot.astype(F32)
        along = jnp.mean(cot * normed, axis=-1, keepdims=True)
        return normed, (inv_rms * (cot - normed * along)).astype(BF16)

    for i in range(N):
        q = q_r[i]
        attn = a_r[i].astype(F32) + dot(q, p_s[i], 1, 0)
        _, out_grad = normalize(attn, g_r[i])
        sg_v[i] = dot(q, out_grad, 0, 0)

    total = sg_v[0]
    for i in range(1, N):
        total += sg_v[i]

    def send_states():
        for i in others:
            send(4, p_s.at[i], p_r.at[me], i).start()

    def home(heads):
        for h in heads:
            c = cols(h)
            q = q_v[:, c]
            state = p_r[h]
            attn = al_v[h] + dot(q, state, 1, 0)
            normed, out_grad = normalize(attn, g_v[:, c])
            n_v[:, c] = normed.astype(BF16)
            grads = dot(out_grad, v_v[:, c], 1, 1)
            grads = jnp.where(causal, grads, F32(0.0)).astype(BF16)
            query_grad = dot(grads, k_v[:, c], 1, 0) + dot(out_grad, state, 1, 1)
            qg_v[:, c] = query_grad.astype(BF16)
            kl_v[h] = dot(grads, q, 0, 0)
            vl_v[h] = dot(sc_v[h], out_grad, 0, 0)

    stores = [
        pltpu.make_async_copy(src, dst, out_sem.at[i])
        for i, (src, dst) in enumerate(
            ((n_v, n_hbm), (qg_v, qg_hbm), (kl_v, kl_hbm), (vl_v, vl_hbm))
        )
    ]

    def early():
        @pl.loop(1, N)
        def _(j):
            arrived(4, p_r, turn(j))

        home(range(N))
        for store in stores:
            store.start()

    later = exchange(True, total, send_states, early)
    for i in range(N - 1, -1, -1):
        t_s[i] = later.astype(BF16)
        later += sg_v[i]
    for i in others:
        send(5, t_s.at[i], t_hbm.at[me], i).start()
    mine_t = pltpu.make_async_copy(t_s.at[me], t_hbm.at[me], self_sem.at[2])
    mine_t.start()

    @pl.loop(1, N)
    def _(j):
        arrived(5, t_hbm, turn(j))

    mine_t.wait()
    for which, buf in enumerate((kv_s, q_r, g_r, a_s, p_s, t_s)):
        all_sent(which, buf)
    exchange_sent(0)
    exchange_sent(1)
    for store in stores:
        store.wait()


def finish(
    n_hbm, qg_hbm, t_hbm, kl_hbm, vl_hbm, k_hbm, v_hbm,
    n_out, qg_out, kg_out, vg_out,
    t_v, kl_v, vl_v, k_v, v_v, kg_v, vg_v, n_v, qg_v,
    in_sem, out_sem, pass_sem,
):
    half = N // PARTS
    loads = []
    for p in range(PARTS):
        heads, wide = pl.ds(p * half, half), pl.ds(p * half * DH, half * DH)
        pairs = (
            (t_hbm.at[heads], t_v.at[heads]),
            (v_hbm.at[:, wide], v_v.at[:, wide]),
            (k_hbm.at[:, wide], k_v.at[:, wide]),
            (kl_hbm.at[heads], kl_v.at[heads]),
            (vl_hbm.at[heads], vl_v.at[heads]),
        )
        loads.append(
            [pltpu.make_async_copy(a, b, in_sem.at[p, i]) for i, (a, b) in enumerate(pairs)]
        )
    passes = [
        pltpu.make_async_copy(n_hbm, n_v, pass_sem.at[0]),
        pltpu.make_async_copy(qg_hbm, qg_v, pass_sem.at[1]),
    ]
    for load in sum(loads, []) + passes:
        load.start()
    stores = [
        pltpu.make_async_copy(n_v, n_out, pass_sem.at[2]),
        pltpu.make_async_copy(qg_v, qg_out, pass_sem.at[3]),
    ]
    for p in range(PARTS):
        for load in loads[p]:
            load.wait()
        for h in range(p * half, (p + 1) * half):
            c = pl.ds(h * DH, DH)
            kg_v[:, c] = (kl_v[h] + dot(v_v[:, c], t_v[h], 1, 1)).astype(BF16)
            vg_v[:, c] = (vl_v[h] + dot(k_v[:, c], t_v[h], 1, 0)).astype(BF16)
        wide = pl.ds(p * half * DH, half * DH)
        for i, (src, dst) in enumerate(((kg_v, kg_out), (vg_v, vg_out))):
            stores.append(
                pltpu.make_async_copy(src.at[:, wide], dst.at[:, wide], out_sem.at[p, i])
            )
            stores[-1].start()
        if p < 2:
            passes[p].wait()
            stores[p].start()
    for store in stores:
        store.wait()


def shards(q, k, v, g):
    tokens, width = q.shape
    wide = pltpu.VMEM((tokens, width), BF16)
    blocks = pltpu.VMEM((N, DH, DH), BF16)
    sums = pltpu.VMEM((N, DH, DH), F32)
    eighths = pltpu.VMEM((2, MEMBERS, DH // MEMBERS, DH), F32)
    groups = pltpu.VMEM((2, GROUPS + 1, DH // MEMBERS, DH), F32)
    dma = pltpu.SemaphoreType.DMA
    whole = jax.ShapeDtypeStruct((tokens, width), BF16)
    states = jax.ShapeDtypeStruct((N, DH, DH), BF16)
    parts = jax.ShapeDtypeStruct((N, DH, DH), F32)
    anywhere = pl.BlockSpec(memory_space=pl.ANY)
    normed, query_grad, later, key_part, value_part = pl.pallas_call(
        kernel,
        out_shape=[whole, whole, states, parts, parts],
        in_specs=[anywhere] * 4,
        out_specs=[anywhere] * 5,
        scratch_shapes=[wide] * 4
        + [blocks] * 9
        + [blocks] + [sums] * 4
        + [wide] * 2
        + [eighths, eighths, groups, eighths, eighths]
        + [dma((4,)), dma((4,)), dma((3,)), dma((6,)), dma((6, N))]
        + [dma((2, 3)), dma((2, GROUPS)), dma((2, MEMBERS)), dma((2, GROUPS)), dma((2, MEMBERS))]
        + [pltpu.SemaphoreType.REGULAR((GROUPS,))],
        compiler_params=pltpu.CompilerParams(
            collective_id=0, has_side_effects=True, vmem_limit_bytes=60 * 1024 * 1024
        ),
        cost_estimate=pl.CostEstimate(
            flops=2 * 12 * N * DH**3, bytes_accessed=16 * tokens * width, transcendentals=0
        ),
    )(q, k, v, g)
    return pl.pallas_call(
        finish,
        out_shape=[whole] * 4,
        in_specs=[anywhere] * 7,
        out_specs=[anywhere] * 4,
        scratch_shapes=[blocks, sums, sums]
        + [wide] * 6
        + [dma((PARTS, 5)), dma((PARTS, 2)), dma((4,))],
        compiler_params=pltpu.CompilerParams(vmem_limit_bytes=60 * 1024 * 1024),
        cost_estimate=pl.CostEstimate(
            flops=2 * 2 * N * DH**3, bytes_accessed=18 * tokens * width, transcendentals=0
        ),
    )(normed, query_grad, later, key_part, value_part, k, v)


def solution(mesh):
    spec = P(("seq", "head"), None)
    return jax.shard_map(
        shards, mesh=mesh, in_specs=(spec,) * 4, out_specs=(spec,) * 4, check_vma=False
    )
```

```python
import jax
import jax.numpy as jnp
from jax import lax
from jax.experimental import pallas as pl
from jax.experimental.pallas import tpu as pltpu
from jax.sharding import PartitionSpec as P

N = 16
DH = 128
PARTS = 2
GROUPS = 8
MEMBERS = 4
EPS = 1e-06
STEPS = (
    (2, 2), (2, 1), (1, 2), (2, 3), (3, 2), (1, 1), (3, 3), (1, 3), (3, 1),
    (2, 0), (0, 2), (1, 0), (0, 1), (3, 0), (0, 3),
)
MESH = pl.DeviceIdType.MESH
F32 = jnp.float32
BF16 = jnp.bfloat16


def dot(a, b, ca, cb):
    return lax.dot_general(a, b, (((ca,), (cb,)), ((), ())), preferred_element_type=F32)


def kernel(
    q_hbm, k_hbm, v_hbm, g_hbm,
    n_hbm, qg_hbm, t_hbm, kl_hbm, vl_hbm,
    q_v, k_v, v_v, g_v,
    kv_s, kv_r, a_s, a_r, q_r, g_r,
    p_s, p_r, t_s,
    sc_v, al_v, sg_v, kl_v, vl_v,
    n_v, qg_v,
    za, zb, zc, zd, ze,
    in_sem, out_sem, self_sem, send_sem, recv_sem,
    zsend_sem, zacross_sem, z1_sem, z2_sem, z3_sem, ready_sem,
):
    me = lax.axis_index("head")
    seq = lax.axis_index("seq")
    group = seq // MEMBERS
    member = seq % MEMBERS

    def plane(i):
        return (i, seq)

    def column(m):
        return (me, group * MEMBERS + m)

    def across(g):
        return (me, g * MEMBERS + member)

    def turn(j):
        return lax.rem(me + j, N)

    def cols(h):
        if isinstance(h, int):
            return pl.ds(h * DH, DH)
        return pl.ds(pl.multiple_of(h * DH, DH), DH)

    y, x = me // 4, me % 4
    others = [lax.rem(y + dy, 4) * 4 + lax.rem(x + dx, 4) for dx, dy in STEPS]

    def peers(reverse):
        for j in range(1, GROUPS):
            g = lax.rem(group + j, GROUPS)
            yield (g, g < group, g > group) if reverse else (g, g > group, g < group)

    barrier = pltpu.get_barrier_semaphore()
    loads = [
        pltpu.make_async_copy(src, dst, in_sem.at[i])
        for i, (src, dst) in enumerate(((k_hbm, k_v), (v_hbm, v_v), (q_hbm, q_v), (g_hbm, g_v)))
    ]
    loads[0].start()
    loads[1].start()
    for i in others:
        pl.semaphore_signal(barrier, inc=1, device_id=plane(i), device_id_type=MESH)
    for g, above, _ in peers(False):

        @pl.when(above)
        def _():
            pl.semaphore_signal(barrier, inc=1, device_id=across(g), device_id_type=MESH)

    for j in range(1, MEMBERS):
        pl.semaphore_signal(
            barrier, inc=1, device_id=column(lax.rem(member + j, MEMBERS)), device_id_type=MESH
        )
    loads[2].start()
    loads[3].start()

    def send(which, src, dst, to):
        return pltpu.make_async_remote_copy(
            src_ref=src,
            dst_ref=dst,
            send_sem=send_sem.at[which],
            recv_sem=recv_sem.at[which, me],
            device_id=plane(to),
            device_id_type=MESH,
        )

    def arrived(which, buf, src):
        pltpu.make_async_remote_copy(
            src_ref=buf.at[src],
            dst_ref=buf.at[src],
            send_sem=send_sem.at[which],
            recv_sem=recv_sem.at[which, src],
            device_id=plane(me),
            device_id_type=MESH,
        ).wait_recv()

    def all_sent(which, buf):
        pltpu.make_async_copy(
            buf.at[pl.ds(0, N - 1)], buf.at[pl.ds(0, N - 1)], send_sem.at[which]
        ).wait()

    loads[0].wait()
    loads[1].wait()

    for h in range(N):
        kv_s[h] = dot(k_v[:, cols(h)], v_v[:, cols(h)], 0, 0).astype(BF16)

    kv_r[me] = kv_s[me]
    pl.semaphore_wait(barrier, N - 1 + MEMBERS - 1 + group)
    for g, _, below in peers(False):

        @pl.when(below)
        def _():
            pl.semaphore_signal(ready_sem.at[group], inc=1, device_id=across(g), device_id_type=MESH)


    for h in others:
        send(0, kv_s.at[h], kv_r.at[me], h).start()

    loads[2].wait()
    loads[3].wait()
    mine_q = pltpu.make_async_copy(q_v.at[:, cols(me)], q_r.at[me], self_sem.at[0])
    mine_g = pltpu.make_async_copy(g_v.at[:, cols(me)], g_r.at[me], self_sem.at[1])
    mine_q.start()
    mine_g.start()

    for h in others:
        send(1, q_v.at[:, cols(h)], q_r.at[me], h).start()
    for h in others:
        send(2, g_v.at[:, cols(h)], g_r.at[me], h).start()

    rows = lax.broadcasted_iota(jnp.int32, (DH, DH), 0)
    causal = rows >= lax.broadcasted_iota(jnp.int32, (DH, DH), 1)

    for h in range(N):
        scores = dot(q_v[:, cols(h)], k_v[:, cols(h)], 1, 1)
        scores = jnp.where(causal, scores, F32(0.0)).astype(BF16)
        sc_v[h] = scores
        local = dot(scores, v_v[:, cols(h)], 1, 0)
        al_v[h] = local
        a_s[h] = local.astype(BF16)
    a_r[me] = a_s[me]

    def across_copy(z, g):
        return pltpu.make_async_remote_copy(
            src_ref=zc.at[z, GROUPS],
            dst_ref=zc.at[z, group],
            send_sem=zacross_sem.at[z, g],
            recv_sem=z2_sem.at[z, group],
            device_id=across(g),
            device_id_type=MESH,
        )

    def exchange(reverse, totals, first, second):
        z = 1 if reverse else 0

        def zsend(step, src, dst, sem, to):
            return pltpu.make_async_remote_copy(
                src_ref=src,
                dst_ref=dst,
                send_sem=zsend_sem.at[z, step],
                recv_sem=sem,
                device_id=to,
                device_id_type=MESH,
            )

        def zwait(dst, sem):
            pltpu.make_async_copy(dst, dst, sem).wait()

        za[z] = totals.reshape(MEMBERS, DH // MEMBERS, DH)
        for j in range(1, MEMBERS):
            m = lax.rem(member + j, MEMBERS)
            zsend(0, za.at[z, m], zb.at[z, member], z1_sem.at[z, member], column(m)).start()
        zb[z, member] = za[z, member]
        first()
        for j in range(1, MEMBERS):
            m = lax.rem(member + j, MEMBERS)
            zwait(zb.at[z, m], z1_sem.at[z, m])
        total = zb[z, 0]
        for m in range(1, MEMBERS):
            total += zb[z, m]
        zc[z, GROUPS] = total.astype(BF16)
        zc[z, group] = jnp.zeros(total.shape, BF16)
        for g, wanted, _ in peers(reverse):

            @pl.when(wanted)
            def _():
                if not reverse:
                    pl.semaphore_wait(ready_sem.at[g], 1)
                across_copy(z, g).start()

        second()
        for g, _, given in peers(reverse):

            @pl.when(given)
            def _():
                zwait(zc.at[z, g], z2_sem.at[z, g])

            @pl.when(jnp.logical_not(given))
            def _():
                zc[z, g] = jnp.zeros(total.shape, BF16)

        running = zc[z, 0].astype(F32)
        for g in range(1, GROUPS):
            running += zc[z, g].astype(F32)
        for m in range(MEMBERS):
            m = MEMBERS - 1 - m if reverse else m
            zd[z, m] = running
            running += zb[z, m]
        for j in range(1, MEMBERS):
            m = lax.rem(member + j, MEMBERS)
            zsend(2, zd.at[z, m], ze.at[z, member], z3_sem.at[z, member], column(m)).start()
        ze[z, member] = zd[z, member]
        for j in range(1, MEMBERS):
            m = lax.rem(member + j, MEMBERS)
            zwait(ze.at[z, m], z3_sem.at[z, m])
        return ze[z].reshape(DH, DH)

    def exchange_sent(z):
        pltpu.make_async_copy(
            za.at[z, pl.ds(0, MEMBERS - 1)], za.at[z, pl.ds(0, MEMBERS - 1)], zsend_sem.at[z, 0]
        ).wait()
        for g, wanted, _ in peers(z == 1):

            @pl.when(wanted)
            def _():
                across_copy(z, g).wait_send()

        pltpu.make_async_copy(
            zd.at[z, pl.ds(0, MEMBERS - 1)], zd.at[z, pl.ds(0, MEMBERS - 1)], zsend_sem.at[z, 2]
        ).wait()

    @pl.loop(1, N)
    def _(j):
        arrived(0, kv_r, turn(j))

    total = kv_r[0].astype(F32)
    for i in range(1, N):
        total += kv_r[i].astype(F32)
    def send_rest():
        for h in others:
            send(3, a_s.at[h], a_r.at[me], h).start()

    state = exchange(False, total, send_rest, lambda: None)
    for i in range(N):
        p_s[i] = state.astype(BF16)
        state += kv_r[i].astype(F32)
    p_r[me] = p_s[me]

    mine_q.wait()
    mine_g.wait()

    @pl.loop(1, N)
    def _(j):
        i = turn(j)
        arrived(1, q_r, i)
        arrived(2, g_r, i)
        arrived(3, a_r, i)

    def normalize(attn, cot):
        inv_rms = lax.rsqrt(jnp.mean(attn * attn, axis=-1, keepdims=True) + EPS)
        normed = attn * inv_rms
        cot = cot.astype(F32)
        along = jnp.mean(cot * normed, axis=-1, keepdims=True)
        return normed, (inv_rms * (cot - normed * along)).astype(BF16)

    for i in range(N):
        q = q_r[i]
        attn = a_r[i].astype(F32) + dot(q, p_s[i], 1, 0)
        _, out_grad = normalize(attn, g_r[i])
        sg_v[i] = dot(q, out_grad, 0, 0)

    total = sg_v[0]
    for i in range(1, N):
        total += sg_v[i]

    def send_states():
        for i in others:
            send(4, p_s.at[i], p_r.at[me], i).start()

    def home(heads):
        for h in heads:
            c = cols(h)
            q = q_v[:, c]
            state = p_r[h]
            attn = al_v[h] + dot(q, state, 1, 0)
            normed, out_grad = normalize(attn, g_v[:, c])
            n_v[:, c] = normed.astype(BF16)
            grads = dot(out_grad, v_v[:, c], 1, 1)
            grads = jnp.where(causal, grads, F32(0.0)).astype(BF16)
            query_grad = dot(grads, k_v[:, c], 1, 0) + dot(out_grad, state, 1, 1)
            qg_v[:, c] = query_grad.astype(BF16)
            kl_v[h] = dot(grads, q, 0, 0)
            vl_v[h] = dot(sc_v[h], out_grad, 0, 0)

    stores = [
        pltpu.make_async_copy(src, dst, out_sem.at[i])
        for i, (src, dst) in enumerate(
            ((n_v, n_hbm), (qg_v, qg_hbm), (kl_v, kl_hbm), (vl_v, vl_hbm))
        )
    ]

    def early():
        @pl.loop(1, N)
        def _(j):
            arrived(4, p_r, turn(j))

        home(range(N))
        for store in stores:
            store.start()

    later = exchange(True, total, send_states, early)
    for i in range(N - 1, -1, -1):
        t_s[i] = later.astype(BF16)
        later += sg_v[i]
    for i in others:
        send(5, t_s.at[i], t_hbm.at[me], i).start()
    mine_t = pltpu.make_async_copy(t_s.at[me], t_hbm.at[me], self_sem.at[2])
    mine_t.start()

    @pl.loop(1, N)
    def _(j):
        arrived(5, t_hbm, turn(j))

    mine_t.wait()
    for which, buf in enumerate((kv_s, q_r, g_r, a_s, p_s, t_s)):
        all_sent(which, buf)
    exchange_sent(0)
    exchange_sent(1)
    for store in stores:
        store.wait()


def finish(
    n_hbm, qg_hbm, t_hbm, kl_hbm, vl_hbm, k_hbm, v_hbm,
    n_out, qg_out, kg_out, vg_out,
    t_v, kl_v, vl_v, k_v, v_v, kg_v, vg_v, n_v, qg_v,
    in_sem, out_sem, pass_sem,
):
    half = N // PARTS
    loads = []
    for p in range(PARTS):
        heads, wide = pl.ds(p * half, half), pl.ds(p * half * DH, half * DH)
        pairs = (
            (t_hbm.at[heads], t_v.at[heads]),
            (v_hbm.at[:, wide], v_v.at[:, wide]),
            (k_hbm.at[:, wide], k_v.at[:, wide]),
            (kl_hbm.at[heads], kl_v.at[heads]),
            (vl_hbm.at[heads], vl_v.at[heads]),
        )
        loads.append(
            [pltpu.make_async_copy(a, b, in_sem.at[p, i]) for i, (a, b) in enumerate(pairs)]
        )
    passes = [
        pltpu.make_async_copy(n_hbm, n_v, pass_sem.at[0]),
        pltpu.make_async_copy(qg_hbm, qg_v, pass_sem.at[1]),
    ]
    for load in sum(loads, []) + passes:
        load.start()
    stores = [
        pltpu.make_async_copy(n_v, n_out, pass_sem.at[2]),
        pltpu.make_async_copy(qg_v, qg_out, pass_sem.at[3]),
    ]
    for p in range(PARTS):
        for load in loads[p]:
            load.wait()
        for h in range(p * half, (p + 1) * half):
            c = pl.ds(h * DH, DH)
            kg_v[:, c] = (kl_v[h] + dot(v_v[:, c], t_v[h], 1, 1)).astype(BF16)
            vg_v[:, c] = (vl_v[h] + dot(k_v[:, c], t_v[h], 1, 0)).astype(BF16)
        wide = pl.ds(p * half * DH, half * DH)
        for i, (src, dst) in enumerate(((kg_v, kg_out), (vg_v, vg_out))):
            stores.append(
                pltpu.make_async_copy(src.at[:, wide], dst.at[:, wide], out_sem.at[p, i])
            )
            stores[-1].start()
        if p < 2:
            passes[p].wait()
            stores[p].start()
    for store in stores:
        store.wait()


def shards(q, k, v, g):
    tokens, width = q.shape
    wide = pltpu.VMEM((tokens, width), BF16)
    blocks = pltpu.VMEM((N, DH, DH), BF16)
    sums = pltpu.VMEM((N, DH, DH), F32)
    quarters = pltpu.VMEM((2, MEMBERS, DH // MEMBERS, DH), F32)
    groups = pltpu.VMEM((2, GROUPS + 1, DH // MEMBERS, DH), BF16)
    dma = pltpu.SemaphoreType.DMA
    whole = jax.ShapeDtypeStruct((tokens, width), BF16)
    states = jax.ShapeDtypeStruct((N, DH, DH), BF16)
    parts = jax.ShapeDtypeStruct((N, DH, DH), F32)
    anywhere = pl.BlockSpec(memory_space=pl.ANY)
    normed, query_grad, later, key_part, value_part = pl.pallas_call(
        kernel,
        out_shape=[whole, whole, states, parts, parts],
        in_specs=[anywhere] * 4,
        out_specs=[anywhere] * 5,
        scratch_shapes=[wide] * 4
        + [blocks] * 9
        + [blocks] + [sums] * 4
        + [wide] * 2
        + [quarters, quarters, groups, quarters, quarters]
        + [dma((4,)), dma((4,)), dma((3,)), dma((6,)), dma((6, N))]
        + [dma((2, 3)), dma((2, GROUPS)), dma((2, MEMBERS)), dma((2, GROUPS)), dma((2, MEMBERS))]
        + [pltpu.SemaphoreType.REGULAR((GROUPS,))],
        compiler_params=pltpu.CompilerParams(
            collective_id=0, has_side_effects=True, vmem_limit_bytes=60 * 1024 * 1024
        ),
        cost_estimate=pl.CostEstimate(
            flops=2 * 12 * N * DH**3, bytes_accessed=16 * tokens * width, transcendentals=0
        ),
    )(q, k, v, g)
    return pl.pallas_call(
        finish,
        out_shape=[whole] * 4,
        in_specs=[anywhere] * 7,
        out_specs=[anywhere] * 4,
        scratch_shapes=[blocks, sums, sums]
        + [wide] * 6
        + [dma((PARTS, 5)), dma((PARTS, 2)), dma((4,))],
        compiler_params=pltpu.CompilerParams(vmem_limit_bytes=60 * 1024 * 1024),
        cost_estimate=pl.CostEstimate(
            flops=2 * 2 * N * DH**3, bytes_accessed=18 * tokens * width, transcendentals=0
        ),
    )(normed, query_grad, later, key_part, value_part, k, v)


def solution(mesh):
    spec = P(("seq", "head"), None)
    return jax.shard_map(
        shards, mesh=mesh, in_specs=(spec,) * 4, out_specs=(spec,) * 4, check_vma=False
    )
```

```python
import jax
import jax.numpy as jnp
from jax import lax
from jax.experimental import pallas as pl
from jax.experimental.pallas import tpu as pltpu
from jax.sharding import PartitionSpec as P

N = 16
DH = 128
PARTS = 2
GROUPS = 8
MEMBERS = 4
EPS = 1e-06
STEPS = (
    (2, 2), (2, 1), (1, 2), (2, 3), (3, 2), (1, 1), (3, 3), (1, 3), (3, 1),
    (2, 0), (0, 2), (1, 0), (0, 1), (3, 0), (0, 3),
)
MESH = pl.DeviceIdType.MESH
F32 = jnp.float32
BF16 = jnp.bfloat16


def dot(a, b, ca, cb):
    return lax.dot_general(a, b, (((ca,), (cb,)), ((), ())), preferred_element_type=F32)


def kernel(
    q_hbm, k_hbm, v_hbm, g_hbm,
    n_hbm, qg_hbm, t_hbm, kl_hbm, vl_hbm,
    q_v, k_v, v_v, g_v,
    kv_s, kv_r, a_s, a_r, q_r, g_r,
    p_s, p_r, t_s,
    sc_v, al_v, sg_v, kl_v, vl_v,
    n_v, qg_v,
    za, zb, zc, zd, ze,
    in_sem, out_sem, self_sem, send_sem, recv_sem,
    zsend_sem, zacross_sem, z1_sem, z2_sem, z3_sem, ready_sem,
):
    me = lax.axis_index("head")
    seq = lax.axis_index("seq")
    group = seq // MEMBERS
    member = seq % MEMBERS

    def plane(i):
        return (i, seq)

    def column(m):
        return (me, group * MEMBERS + m)

    def across(g):
        return (me, g * MEMBERS + member)

    def cols(h):
        if isinstance(h, int):
            return pl.ds(h * DH, DH)
        return pl.ds(pl.multiple_of(h * DH, DH), DH)

    y, x = me // 4, me % 4
    others = [lax.rem(y + dy, 4) * 4 + lax.rem(x + dx, 4) for dx, dy in STEPS]

    def peers(reverse):
        for j in (4, 3, 5, 2, 6, 1, 7):
            g = lax.rem(group + j, GROUPS)
            yield (g, g < group, g > group) if reverse else (g, g > group, g < group)

    barrier = pltpu.get_barrier_semaphore()
    loads = [
        pltpu.make_async_copy(src, dst, in_sem.at[i])
        for i, (src, dst) in enumerate(((k_hbm, k_v), (v_hbm, v_v), (q_hbm, q_v), (g_hbm, g_v)))
    ]
    loads[0].start()
    loads[1].start()
    for i in others:
        pl.semaphore_signal(barrier, inc=1, device_id=plane(i), device_id_type=MESH)
    for g, above, _ in peers(False):

        @pl.when(above)
        def _():
            pl.semaphore_signal(barrier, inc=1, device_id=across(g), device_id_type=MESH)

    for j in range(1, MEMBERS):
        pl.semaphore_signal(
            barrier, inc=1, device_id=column(lax.rem(member + j, MEMBERS)), device_id_type=MESH
        )
    loads[2].start()
    loads[3].start()

    def send(which, src, dst, to):
        return pltpu.make_async_remote_copy(
            src_ref=src,
            dst_ref=dst,
            send_sem=send_sem.at[which],
            recv_sem=recv_sem.at[which],
            device_id=plane(to),
            device_id_type=MESH,
        )

    def arrived(which, buf):
        pltpu.make_async_copy(
            buf.at[pl.ds(0, N - 1)], buf.at[pl.ds(0, N - 1)], recv_sem.at[which]
        ).wait()

    def all_sent(which, buf):
        pltpu.make_async_copy(
            buf.at[pl.ds(0, N - 1)], buf.at[pl.ds(0, N - 1)], send_sem.at[which]
        ).wait()

    loads[0].wait()
    loads[1].wait()

    for h in range(N):
        kv_s[h] = dot(k_v[:, cols(h)], v_v[:, cols(h)], 0, 0).astype(BF16)

    kv_r[me] = kv_s[me]
    pl.semaphore_wait(barrier, N - 1 + MEMBERS - 1 + group)
    for g, _, below in peers(False):

        @pl.when(below)
        def _():
            pl.semaphore_signal(ready_sem.at[group], inc=1, device_id=across(g), device_id_type=MESH)


    for h in others:
        send(0, kv_s.at[h], kv_r.at[me], h).start()

    loads[2].wait()
    loads[3].wait()
    mine_q = pltpu.make_async_copy(q_v.at[:, cols(me)], q_r.at[me], self_sem.at[0])
    mine_g = pltpu.make_async_copy(g_v.at[:, cols(me)], g_r.at[me], self_sem.at[1])
    mine_q.start()
    mine_g.start()

    for h in others:
        send(1, q_v.at[:, cols(h)], q_r.at[me], h).start()

    rows = lax.broadcasted_iota(jnp.int32, (DH, DH), 0)
    causal = rows >= lax.broadcasted_iota(jnp.int32, (DH, DH), 1)

    for h in range(N):
        scores = dot(q_v[:, cols(h)], k_v[:, cols(h)], 1, 1)
        scores = jnp.where(causal, scores, F32(0.0)).astype(BF16)
        sc_v[h] = scores
        local = dot(scores, v_v[:, cols(h)], 1, 0)
        al_v[h] = local
        a_s[h] = local.astype(BF16)
    a_r[me] = a_s[me]

    def across_copy(z, g):
        return pltpu.make_async_remote_copy(
            src_ref=zc.at[z, GROUPS],
            dst_ref=zc.at[z, group],
            send_sem=zacross_sem.at[z, g],
            recv_sem=z2_sem.at[z, group],
            device_id=across(g),
            device_id_type=MESH,
        )

    def exchange(reverse, totals, first, second):
        z = 1 if reverse else 0

        def zsend(step, src, dst, sem, to):
            return pltpu.make_async_remote_copy(
                src_ref=src,
                dst_ref=dst,
                send_sem=zsend_sem.at[z, step],
                recv_sem=sem,
                device_id=to,
                device_id_type=MESH,
            )

        def zwait(dst, sem):
            pltpu.make_async_copy(dst, dst, sem).wait()

        za[z] = totals.reshape(MEMBERS, DH // MEMBERS, DH)
        for j in range(1, MEMBERS):
            m = lax.rem(member + j, MEMBERS)
            zsend(0, za.at[z, m], zb.at[z, member], z1_sem.at[z, member], column(m)).start()
        zb[z, member] = za[z, member]
        first()
        for j in range(1, MEMBERS):
            m = lax.rem(member + j, MEMBERS)
            zwait(zb.at[z, m], z1_sem.at[z, m])
        total = zb[z, 0]
        for m in range(1, MEMBERS):
            total += zb[z, m]
        zc[z, GROUPS] = total.astype(BF16)
        zc[z, group] = jnp.zeros(total.shape, BF16)
        for g, wanted, _ in peers(reverse):

            @pl.when(wanted)
            def _():
                if not reverse:
                    pl.semaphore_wait(ready_sem.at[g], 1)
                across_copy(z, g).start()

        second()
        for g, _, given in peers(reverse):

            @pl.when(given)
            def _():
                zwait(zc.at[z, g], z2_sem.at[z, g])

            @pl.when(jnp.logical_not(given))
            def _():
                zc[z, g] = jnp.zeros(total.shape, BF16)

        running = zc[z, 0].astype(F32)
        for g in range(1, GROUPS):
            running += zc[z, g].astype(F32)
        for m in range(MEMBERS):
            m = MEMBERS - 1 - m if reverse else m
            zd[z, m] = running
            running += zb[z, m]
        for j in range(1, MEMBERS):
            m = lax.rem(member + j, MEMBERS)
            zsend(2, zd.at[z, m], ze.at[z, member], z3_sem.at[z, member], column(m)).start()
        ze[z, member] = zd[z, member]
        for j in range(1, MEMBERS):
            m = lax.rem(member + j, MEMBERS)
            zwait(ze.at[z, m], z3_sem.at[z, m])
        return ze[z].reshape(DH, DH)

    def exchange_sent(z):
        pltpu.make_async_copy(
            za.at[z, pl.ds(0, MEMBERS - 1)], za.at[z, pl.ds(0, MEMBERS - 1)], zsend_sem.at[z, 0]
        ).wait()
        for g, wanted, _ in peers(z == 1):

            @pl.when(wanted)
            def _():
                across_copy(z, g).wait_send()

        pltpu.make_async_copy(
            zd.at[z, pl.ds(0, MEMBERS - 1)], zd.at[z, pl.ds(0, MEMBERS - 1)], zsend_sem.at[z, 2]
        ).wait()

    arrived(0, kv_r)

    total = kv_r[0].astype(F32)
    for i in range(1, N):
        total += kv_r[i].astype(F32)
    def send_rest():
        for h in others:
            send(2, g_v.at[:, cols(h)], g_r.at[me], h).start()
        for h in others:
            send(3, a_s.at[h], a_r.at[me], h).start()

    state = exchange(False, total, send_rest, lambda: None)
    for i in range(N):
        p_s[i] = state.astype(BF16)
        state += kv_r[i].astype(F32)
    p_r[me] = p_s[me]

    mine_q.wait()
    mine_g.wait()

    arrived(1, q_r)
    arrived(2, g_r)
    arrived(3, a_r)

    def normalize(attn, cot):
        inv_rms = lax.rsqrt(jnp.mean(attn * attn, axis=-1, keepdims=True) + EPS)
        normed = attn * inv_rms
        cot = cot.astype(F32)
        along = jnp.mean(cot * normed, axis=-1, keepdims=True)
        return normed, (inv_rms * (cot - normed * along)).astype(BF16)

    for i in range(N):
        q = q_r[i]
        attn = a_r[i].astype(F32) + dot(q, p_s[i], 1, 0)
        _, out_grad = normalize(attn, g_r[i])
        sg_v[i] = dot(q, out_grad, 0, 0)

    total = sg_v[0]
    for i in range(1, N):
        total += sg_v[i]

    def send_states():
        for i in others:
            send(4, p_s.at[i], p_r.at[me], i).start()

    def home(heads):
        for h in heads:
            c = cols(h)
            q = q_v[:, c]
            state = p_r[h]
            attn = al_v[h] + dot(q, state, 1, 0)
            normed, out_grad = normalize(attn, g_v[:, c])
            n_v[:, c] = normed.astype(BF16)
            grads = dot(out_grad, v_v[:, c], 1, 1)
            grads = jnp.where(causal, grads, F32(0.0)).astype(BF16)
            query_grad = dot(grads, k_v[:, c], 1, 0) + dot(out_grad, state, 1, 1)
            qg_v[:, c] = query_grad.astype(BF16)
            kl_v[h] = dot(grads, q, 0, 0)
            vl_v[h] = dot(sc_v[h], out_grad, 0, 0)

    stores = [
        pltpu.make_async_copy(src, dst, out_sem.at[i])
        for i, (src, dst) in enumerate(
            ((n_v, n_hbm), (qg_v, qg_hbm), (kl_v, kl_hbm), (vl_v, vl_hbm))
        )
    ]

    def early():
        after = jnp.zeros((DH, DH), F32)
        for i in range(N - 1, -1, -1):
            mine = sg_v[i]
            sg_v[i] = after
            after += mine
        arrived(4, p_r)

        home(range(N))
        for store in stores:
            store.start()

    later = exchange(True, total, send_states, early)
    for i in others:
        t_s[i] = (sg_v[i] + later).astype(BF16)
        send(5, t_s.at[i], t_hbm.at[me], i).start()
    t_s[me] = (sg_v[me] + later).astype(BF16)
    mine_t = pltpu.make_async_copy(t_s.at[me], t_hbm.at[me], self_sem.at[2])
    mine_t.start()

    arrived(5, t_hbm)

    mine_t.wait()
    for which, buf in enumerate((kv_s, q_r, g_r, a_s, p_s, t_s)):
        all_sent(which, buf)
    exchange_sent(0)
    exchange_sent(1)
    for store in stores:
        store.wait()


def finish(
    n_hbm, qg_hbm, t_hbm, kl_hbm, vl_hbm, k_hbm, v_hbm,
    n_out, qg_out, kg_out, vg_out,
    t_v, kl_v, vl_v, k_v, v_v, kg_v, vg_v, n_v, qg_v,
    in_sem, out_sem, pass_sem,
):
    half = N // PARTS
    loads = []
    for p in range(PARTS):
        heads, wide = pl.ds(p * half, half), pl.ds(p * half * DH, half * DH)
        pairs = (
            (t_hbm.at[heads], t_v.at[heads]),
            (v_hbm.at[:, wide], v_v.at[:, wide]),
            (k_hbm.at[:, wide], k_v.at[:, wide]),
            (kl_hbm.at[heads], kl_v.at[heads]),
            (vl_hbm.at[heads], vl_v.at[heads]),
        )
        loads.append(
            [pltpu.make_async_copy(a, b, in_sem.at[p, i]) for i, (a, b) in enumerate(pairs)]
        )
    passes = [
        pltpu.make_async_copy(n_hbm, n_v, pass_sem.at[0]),
        pltpu.make_async_copy(qg_hbm, qg_v, pass_sem.at[1]),
    ]
    for load in sum(loads, []) + passes:
        load.start()
    stores = [
        pltpu.make_async_copy(n_v, n_out, pass_sem.at[2]),
        pltpu.make_async_copy(qg_v, qg_out, pass_sem.at[3]),
    ]
    for p in range(PARTS):
        for load in loads[p]:
            load.wait()
        for h in range(p * half, (p + 1) * half):
            c = pl.ds(h * DH, DH)
            kg_v[:, c] = (kl_v[h] + dot(v_v[:, c], t_v[h], 1, 1)).astype(BF16)
            vg_v[:, c] = (vl_v[h] + dot(k_v[:, c], t_v[h], 1, 0)).astype(BF16)
        wide = pl.ds(p * half * DH, half * DH)
        for i, (src, dst) in enumerate(((kg_v, kg_out), (vg_v, vg_out))):
            stores.append(
                pltpu.make_async_copy(src.at[:, wide], dst.at[:, wide], out_sem.at[p, i])
            )
            stores[-1].start()
        if p < 2:
            passes[p].wait()
            stores[p].start()
    for store in stores:
        store.wait()


def shards(q, k, v, g):
    tokens, width = q.shape
    wide = pltpu.VMEM((tokens, width), BF16)
    blocks = pltpu.VMEM((N, DH, DH), BF16)
    sums = pltpu.VMEM((N, DH, DH), F32)
    quarters = pltpu.VMEM((2, MEMBERS, DH // MEMBERS, DH), F32)
    groups = pltpu.VMEM((2, GROUPS + 1, DH // MEMBERS, DH), BF16)
    dma = pltpu.SemaphoreType.DMA
    whole = jax.ShapeDtypeStruct((tokens, width), BF16)
    states = jax.ShapeDtypeStruct((N, DH, DH), BF16)
    parts = jax.ShapeDtypeStruct((N, DH, DH), F32)
    anywhere = pl.BlockSpec(memory_space=pl.ANY)
    normed, query_grad, later, key_part, value_part = pl.pallas_call(
        kernel,
        out_shape=[whole, whole, states, parts, parts],
        in_specs=[anywhere] * 4,
        out_specs=[anywhere] * 5,
        scratch_shapes=[wide] * 4
        + [blocks] * 9
        + [blocks] + [sums] * 4
        + [wide] * 2
        + [quarters, quarters, groups, quarters, quarters]
        + [dma((4,)), dma((4,)), dma((3,)), dma((6,)), dma((6,))]
        + [dma((2, 3)), dma((2, GROUPS)), dma((2, MEMBERS)), dma((2, GROUPS)), dma((2, MEMBERS))]
        + [pltpu.SemaphoreType.REGULAR((GROUPS,))],
        compiler_params=pltpu.CompilerParams(
            collective_id=0, has_side_effects=True, vmem_limit_bytes=60 * 1024 * 1024
        ),
        cost_estimate=pl.CostEstimate(
            flops=2 * 12 * N * DH**3, bytes_accessed=16 * tokens * width, transcendentals=0
        ),
    )(q, k, v, g)
    return pl.pallas_call(
        finish,
        out_shape=[whole] * 4,
        in_specs=[anywhere] * 7,
        out_specs=[anywhere] * 4,
        scratch_shapes=[blocks, sums, sums]
        + [wide] * 6
        + [dma((PARTS, 5)), dma((PARTS, 2)), dma((4,))],
        compiler_params=pltpu.CompilerParams(vmem_limit_bytes=60 * 1024 * 1024),
        cost_estimate=pl.CostEstimate(
            flops=2 * 2 * N * DH**3, bytes_accessed=18 * tokens * width, transcendentals=0
        ),
    )(normed, query_grad, later, key_part, value_part, k, v)


def solution(mesh):
    spec = P(("seq", "head"), None)
    return jax.shard_map(
        shards, mesh=mesh, in_specs=(spec,) * 4, out_specs=(spec,) * 4, check_vma=False
    )
```
